256 devices in a mesh: grp: 4 (over x), row: 64 (over z, y, core).
Axes of the slice: x: 4, y: 4, z: 8, core: 2. Of those that a mesh axis runs over, the one named last changes fastest.
Arguments:
- vectors: bfloat16 [64, 2048, 128], P('row', 'grp'), may hold values from -48 to 48
- tangent: bfloat16 [64, 1152, 128, 128], P('row', 'grp'), may hold values from -0.109375 to 0.109375
- block_cols: int32 [64, 1152], P('row', 'grp'), may hold values from 0 to 1023, as said below
- dest_blocks: int32 [64, 1152], P('row', 'grp'), may hold values from 0 to 1023, as said below
- live_slots: int32 [64, 4], P('row', 'grp'), may hold values from 1 to 288, as said below
Outputs:
- images: bfloat16 [64, 2048, 128], P('row', 'grp')
- gram: float32 [128, 128], replicated
The draws below stay inside these ranges and needn't reach their ends.
Inputs may be any that keep to these rules, and one draw needn't show every extreme that they name: `block_cols`: every slot of slab r has its block column in slab r, from 4 * 4 * r to 4 * 4 * (r + 1) - 1. `dest_blocks`: every slot of slab r, live or not, names a block row of slab r - 1, r or r + 1. `live_slots`: the live slots of an index of grp are its first ones; in every draw some index of grp of some slab has all 288 slots live.
All inputs are finite; a program needn't handle non-finite values.
Results may differ from the reference program's by a relative error of at most 0.001.
Values may be sent and summed in bfloat16 or wider, within the bound.
No kernel may reach another device: no remote copies, remote signals or barrier semaphores. Data moves between devices by JAX's collectives and lax.ppermute only.
A program may use at most 64 MiB of HBM per device.

```python
import math
import jax
import jax.numpy as jnp
from jax import lax

BS = 128
KR = 128
VB_DEV = 4
NNZ_DEV = 288
SLAB_ROWS = 2048
NBR = 1024
SLOTS = 1152
N_GRP = 4
N_ROW = 64


def draw_vectors(key, part):
    key = jax.random.fold_in(key, 11)
    key_entries, key_scales = jax.random.split(key, 2)
    slab_pos = jnp.arange(N_ROW, dtype=jnp.float32)[:, None, None] / float(N_ROW - 1)
    slab_rise = 1.0 + 2.0 * slab_pos
    entries = jax.random.normal(key_entries, (N_ROW, SLAB_ROWS, KR), jnp.float32)
    scales = jnp.exp(jax.random.uniform(key_scales, (N_ROW, SLAB_ROWS, 1), jnp.float32, 0.0, 2.3025851))
    return (entries * scales * slab_rise / 6.0).astype(jnp.bfloat16)


def draw_block_cols(key, part):
    key = jax.random.fold_in(key, 23)
    slab_blocks = VB_DEV * N_GRP
    first_col = jnp.arange(N_ROW, dtype=jnp.int32)[:, None] * slab_blocks
    return first_col + jax.random.randint(key, (N_ROW, SLOTS), 0, slab_blocks, jnp.int32)


def draw_dest_blocks(key, part):
    key = jax.random.fold_in(key, 37)
    slab_blocks = VB_DEV * N_GRP
    slab_index = jnp.arange(N_ROW, dtype=jnp.int32)[:, None]
    lowest = jnp.where(slab_index == 0, 0, -slab_blocks).astype(jnp.int32)
    highest = jnp.where(slab_index == N_ROW - 1, slab_blocks, 2 * slab_blocks).astype(jnp.int32)
    offsets = jax.random.randint(key, (N_ROW, SLOTS), lowest, highest, jnp.int32)
    return slab_index * slab_blocks + offsets


def draw_live_slots(key, part):
    key = jax.random.fold_in(key, 41)
    key_counts, key_full = jax.random.split(key)
    raw_draw = jax.random.randint(key_counts, (N_ROW, N_GRP), 1, NNZ_DEV + 1, jnp.int32)
    counts = jnp.maximum(raw_draw * raw_draw // NNZ_DEV, 1)
    full_device = jax.random.randint(key_full, (), 0, N_ROW * N_GRP, jnp.int32)
    device_ids = jnp.arange(N_ROW * N_GRP, dtype=jnp.int32).reshape(N_ROW, N_GRP)
    return jnp.where(device_ids == full_device, NNZ_DEV, counts).astype(jnp.int32)


def levels(stream_key, extent, shards, least, largest):
    def one(position, shards_of):
        steps = jax.random.uniform(jax.random.fold_in(jax.random.fold_in(stream_key, 6), position), (shards_of,), jnp.float32, least / len(shards), largest / len(shards))
        return jnp.repeat(jnp.exp(steps), extent[position] // shards_of).reshape((-1,) + (1,) * (len(extent) - position - 1))

    gain = one(*shards[0])
    for cut in shards[1:]:
        gain = gain * one(*cut)
    return gain


def scatter_about(stream_key, extent, spread, most, pieces=(), kind=jnp.bfloat16):
    result = jax.random.normal(stream_key, extent, jnp.float32) * spread
    if len(pieces) > 0:
        result = levels(stream_key, extent, pieces, -0.22, 0.18) * result
    return jnp.clip(result, min=-most, max=most).astype(kind)


def setup_inputs(seed: int = 0) -> dict:
    key_of = jax.random.split(jax.random.key(seed), 6)
    return {
        "vectors": draw_vectors(jax.random.fold_in(key_of[5], 71), 0),
        "tangent": scatter_about(key_of[1], (N_ROW, SLOTS, BS, BS), (BS * NNZ_DEV // (3 * VB_DEV)) ** -0.5, 0.109375, ((0, 64), (1, 4))),
        "block_cols": draw_block_cols(jax.random.fold_in(key_of[5], 71), 0),
        "dest_blocks": draw_dest_blocks(jax.random.fold_in(key_of[5], 71), 0),
        "live_slots": draw_live_slots(jax.random.fold_in(key_of[5], 71), 0),
    }


def reference(vectors, tangent, block_cols, dest_blocks, live_slots):
    basis_blocks = vectors.reshape(NBR, BS, KR)
    slot_ids = jnp.arange(SLOTS, dtype=jnp.int32)
    owner_grp = slot_ids // NNZ_DEV
    local_slot = slot_ids % NNZ_DEV

    def one_slab(image_sum, inputs):
        tile_rows, col_ids, dest_ids, counts = inputs
        live_mask = (local_slot < counts[owner_grp]).astype(jnp.float32)
        picked = jnp.take(basis_blocks, col_ids, axis=0).astype(jnp.float32)
        products = jnp.einsum('sij,sjk->sik', tile_rows.astype(jnp.float32), picked)
        products = products * live_mask[:, None, None]
        return (image_sum.at[dest_ids].add(products), None)
    start_sum = jnp.zeros((NBR, BS, KR), jnp.float32)
    image_sum, unused = lax.scan(one_slab, start_sum, (tangent, block_cols, dest_blocks, live_slots))
    images = image_sum.astype(jnp.bfloat16).reshape(N_ROW, SLAB_ROWS, KR)
    flat_vectors = vectors.reshape(NBR * BS, KR).astype(jnp.float32)
    flat_images = image_sum.reshape(NBR * BS, KR)
    gram = jnp.dot(flat_vectors.T, flat_images, precision=lax.Precision.HIGHEST, preferred_element_type=jnp.float32)
    gram = gram * (1.0 / math.sqrt(NBR * BS))
    return (images, gram)
```

```python
import math

import jax
import jax.numpy as jnp
from jax import lax
from jax.experimental import pallas as pl
from jax.experimental.pallas import tpu as pltpu
from jax.sharding import PartitionSpec as P

BS = 128
KR = 128
VB_DEV = 4
NNZ_DEV = 288
GRP = 4
SLAB_BLOCKS = VB_DEV * GRP
WINDOW = 3 * SLAB_BLOCKS
CHUNK = 32
GROUP = 32
F32 = jnp.float32
BF16 = jnp.bfloat16
VMEM = pl.BlockSpec(memory_space=pltpu.VMEM)
SMEM = pl.BlockSpec(memory_space=pltpu.SMEM)


def passed_along(value, axis, steps):
    count = lax.axis_size(axis)
    initial, last = (max(0, -steps), min(count, count - steps))
    return lax.ppermute(value, axis, [(source, source + steps) for source in range(initial, last)])


def turned(value, axis, steps):
    count = lax.axis_size(axis)
    return lax.ppermute(value, axis, [(source, (source + steps) % count) for source in range(count)])


def row_moved(value, target):
    return lax.ppermute(value, "row", [(source, target(source)) for source in range(64)])


def core_swapped(value):
    return row_moved(value, lambda r: r ^ 1)


def y_turned(value, steps):
    return row_moved(value, lambda r: r // 8 * 8 + (r // 2 + steps) % 4 * 2 + r % 2)


def z_turned(value, steps):
    return row_moved(value, lambda r: (r // 8 + steps) % 8 * 8 + r % 8)


def pack_kernel(place, own, one, two, three, basis, basis_t):
    for steps, shard in enumerate((own, one, two, three)):
        at = (place[0] - steps) & (GRP - 1)
        for block in range(VB_DEV):
            value = shard[pl.ds(block * BS, BS), :]
            basis[at * VB_DEV + block] = value
            basis_t[at * VB_DEV + block] = value.T


def slots_kernel(cols, dests, live, basis, tangent, window, held, sems):
    count = live[0, 0]

    def copy(index):
        part = pl.ds(index * CHUNK, CHUNK)
        return pltpu.make_async_copy(tangent.at[part], held.at[part], sems.at[index])

    def start(index, carry):
        copy(index).start()
        return carry

    lax.fori_loop(0, (count + CHUNK - 1) // CHUNK, start, 0)
    window[...] = jnp.zeros_like(window)
    window_base = (cols[0, 0] & -SLAB_BLOCKS) - SLAB_BLOCKS

    def group(index, carry):
        copy(index).wait()
        for offset in range(GROUP):
            slot = index * GROUP + offset
            product = jnp.dot(
                held[slot], basis[cols[0, slot] & (SLAB_BLOCKS - 1)], preferred_element_type=F32
            )
            dest = jnp.where(slot < count, dests[0, slot] - window_base, WINDOW)
            window[dest] += product
        return carry

    lax.fori_loop(0, (count + GROUP - 1) // GROUP, group, 0)


def gram_kernel(window, below_t, own_t, above_t, gram, down, up):
    total = jnp.zeros((KR, 2 * KR), F32)
    for part, basis_t in enumerate((below_t, own_t, above_t)):
        for block in range(SLAB_BLOCKS):
            value = window[part * SLAB_BLOCKS + block]
            if part == 0:
                down[block] = value
            if part == 2:
                up[block] = value
            high = value.astype(BF16)
            low = (value - high.astype(F32)).astype(BF16)
            total += jnp.dot(
                basis_t[block], jnp.concatenate([high, low], axis=1), preferred_element_type=F32
            )
    gram[...] = total[:, :KR] + total[:, KR:]


def body(vectors, tangent, block_cols, dest_blocks, live_slots):
    grp_index = lax.axis_index("grp")
    core = lax.axis_index("row") % 2
    own = vectors.reshape(VB_DEV * BS, KR)
    shards = [own] + [turned(own, "grp", steps) for steps in (1, 2, 3)]
    slab = jax.ShapeDtypeStruct((SLAB_BLOCKS, BS, KR), BF16)
    slab_f32 = jax.ShapeDtypeStruct((SLAB_BLOCKS, BS, KR), F32)
    basis, basis_t = pl.pallas_call(
        pack_kernel,
        out_shape=(slab, slab),
        in_specs=[SMEM] + [VMEM] * 4,
        out_specs=(VMEM, VMEM),
    )(grp_index.reshape(1), *shards)
    above_t = passed_along(basis_t, "row", -1)
    below_t = passed_along(basis_t, "row", 1)
    window = pl.pallas_call(
        slots_kernel,
        out_shape=jax.ShapeDtypeStruct((WINDOW + 1, BS, KR), F32),
        in_specs=[SMEM] * 3 + [VMEM, pl.BlockSpec(memory_space=pl.ANY)],
        out_specs=VMEM,
        scratch_shapes=[
            pltpu.VMEM((NNZ_DEV, BS, BS), BF16),
            pltpu.SemaphoreType.DMA((NNZ_DEV // CHUNK,)),
        ],
        compiler_params=pltpu.CompilerParams(vmem_limit_bytes=32 << 20),
    )(block_cols, dest_blocks, live_slots, basis, tangent.reshape(NNZ_DEV, BS, BS))
    gram, down, up = pl.pallas_call(
        gram_kernel,
        out_shape=(jax.ShapeDtypeStruct((KR, KR), F32), slab_f32, slab_f32),
        in_specs=[VMEM] * 4,
        out_specs=(VMEM, VMEM, VMEM),
        compiler_params=pltpu.CompilerParams(vmem_limit_bytes=32 << 20),
    )(window, below_t, basis_t, above_t)

    above_part = passed_along(down, "row", -1)
    below_part = passed_along(up, "row", 1)

    half = KR // 2
    kept = lax.dynamic_slice_in_dim(gram, core * half, half, 0)
    given = lax.dynamic_slice_in_dim(gram, (1 - core) * half, half, 0)
    term = kept + core_swapped(given)
    term = term + turned(term, "grp", 1) + turned(term, "grp", 2) + turned(term, "grp", 3)
    term = term + y_turned(term, 1) + y_turned(term, 2) + y_turned(term, 3)
    term = term + z_turned(term, 2) + z_turned(term, 4) + z_turned(term, 6)
    term = term + row_moved(term, lambda r: r ^ 8)
    term = term * (1.0 / math.sqrt(VB_DEV * BS * GRP * lax.axis_size("row")))
    other = core_swapped(term)
    gram = jnp.where(core == 0, jnp.concatenate([term, other]), jnp.concatenate([other, term]))

    slab_sum = window[SLAB_BLOCKS : 2 * SLAB_BLOCKS] + above_part + below_part

    def piece(steps):
        first = (grp_index + steps) % GRP * VB_DEV
        return lax.dynamic_slice_in_dim(slab_sum, first, VB_DEV, 0)

    owned_sum = piece(0)
    for steps in (1, 2, 3):
        owned_sum = owned_sum + turned(piece(steps), "grp", steps)
    images = owned_sum.astype(BF16).reshape(1, VB_DEV * BS, KR)
    return (images, gram)


def solution(mesh):
    return jax.shard_map(
        body,
        mesh=mesh,
        in_specs=(
            P("row", "grp", None),
            P("row", "grp", None, None),
            P("row", "grp"),
            P("row", "grp"),
            P("row", "grp"),
        ),
        out_specs=(P("row", "grp", None), P()),
        check_vma=False,
    )
```

```python
import math

import jax
import jax.numpy as jnp
from jax import lax
from jax.experimental import pallas as pl
from jax.experimental.pallas import tpu as pltpu
from jax.sharding import PartitionSpec as P

BS = 128
KR = 128
VB_DEV = 4
NNZ_DEV = 288
GRP = 4
SLAB_BLOCKS = VB_DEV * GRP
WINDOW = 3 * SLAB_BLOCKS
GROUP = 48
F32 = jnp.float32
BF16 = jnp.bfloat16
VMEM = pl.BlockSpec(memory_space=pltpu.VMEM)
SMEM = pl.BlockSpec(memory_space=pltpu.SMEM)


def turned(value, axis, steps):
    count = lax.axis_size(axis)
    return lax.ppermute(value, axis, [(source, (source + steps) % count) for source in range(count)])


def row_moved(value, target):
    return lax.ppermute(value, "row", [(source, target(source)) for source in range(64)])


def core_swapped(value):
    return row_moved(value, lambda r: r ^ 1)


def far_swapped(value):
    return lax.ppermute(value, "row", [(r, r + 1 if r % 2 else r - 1) for r in range(1, 63)])


def y_turned(value, steps):
    return row_moved(value, lambda r: r // 8 * 8 + (r // 2 + steps) % 4 * 2 + r % 2)


def z_paired(value, target):
    return row_moved(value, lambda r: target(r // 8) * 8 + r % 8)


def stay_kernel(own, held):
    held[...] = own[...]


def turn_kernel(own, one, two, three, basis_t):
    place = lax.axis_index("grp")
    for steps, shard in enumerate((own, one, two, three)):
        at = (place - steps) & (GRP - 1)
        for block in range(VB_DEV):
            basis_t[at * VB_DEV + block] = shard[pl.ds(block * BS, BS), :].T


def slots_kernel(codes, own, one, two, three, tangent, window, basis, held, sems):
    place = lax.axis_index("grp")
    groups = (codes[0, NNZ_DEV] + GROUP - 1) // GROUP

    def copy(index):
        part = pl.ds(index * GROUP, GROUP)
        return pltpu.make_async_copy(tangent.at[part], held.at[part], sems.at[index])

    def start(index, carry):
        copy(index).start()
        return carry

    lax.fori_loop(0, groups, start, 0)
    for steps, shard in enumerate((own, one, two, three)):
        at = (place - steps) & (GRP - 1)
        for block in range(VB_DEV):
            basis[at * VB_DEV + block] = shard[pl.ds(block * BS, BS), :]
    window[...] = jnp.zeros_like(window)

    def group(index, carry):
        copy(index).wait()
        for offset in range(GROUP):
            slot = index * GROUP + offset
            code = codes[0, slot]
            window[code // SLAB_BLOCKS] += jnp.dot(
                held[slot], basis[code % SLAB_BLOCKS], preferred_element_type=F32
            )
        return carry

    lax.fori_loop(0, groups, group, 0)


def gram_kernel(window, near_t, own_t, far_t, gram_kept, gram_given, near, far):
    core = lax.axis_index("row") & 1
    near_at = (1 - core) * (2 * SLAB_BLOCKS)
    far_at = core * (2 * SLAB_BLOCKS)
    total = jnp.zeros((KR, 2 * KR), F32)
    for first, basis_t, sent in ((SLAB_BLOCKS, own_t, None), (near_at, near_t, near), (far_at, far_t, far)):
        for block in range(SLAB_BLOCKS):
            value = window[first + block]
            if sent is not None:
                sent[block] = value
            high = value.astype(BF16)
            low = (value - high.astype(F32)).astype(BF16)
            total += jnp.dot(
                basis_t[block], jnp.concatenate([high, low], axis=1), preferred_element_type=F32
            )
    gram = total[:, :KR] + total[:, KR:]
    half = KR // 2
    first = core == 0
    gram_kept[...] = jnp.where(first, gram[:half], gram[half:])
    gram_given[...] = jnp.where(first, gram[half:], gram[:half])


def pieces_kernel(window, near, far, own, one, two, three):
    place = lax.axis_index("grp")
    for steps, piece in enumerate((own, one, two, three)):
        at = ((place + steps) & (GRP - 1)) * VB_DEV
        for block in range(VB_DEV):
            piece[block] = window[SLAB_BLOCKS + at + block] + near[at + block] + far[at + block]


def shape(*sizes, dtype=F32):
    return jax.ShapeDtypeStruct(sizes, dtype)


def body(vectors, tangent, block_cols, dest_blocks, live_slots):
    core = lax.axis_index("row") % 2
    own = vectors.reshape(VB_DEV * BS, KR)
    shards = [turned(own, "grp", steps) for steps in (1, 2, 3)]

    window_base = (lax.axis_index("row") - 1) * SLAB_BLOCKS
    live = lax.broadcasted_iota(jnp.int32, (1, NNZ_DEV), 1) < live_slots
    places = jnp.where(live, dest_blocks - window_base, WINDOW)
    codes = places * SLAB_BLOCKS + (block_cols & (SLAB_BLOCKS - 1))
    codes = jnp.concatenate([codes, live_slots], axis=1)
    own = pl.pallas_call(
        stay_kernel,
        out_shape=shape(VB_DEV * BS, KR, dtype=BF16),
        in_specs=[VMEM],
        out_specs=VMEM,
        compiler_params=pltpu.CompilerParams(vmem_limit_bytes=8 << 20),
    )(own)
    codes, *shards = lax.optimization_barrier((codes, own, *shards))

    basis_t = pl.pallas_call(
        turn_kernel,
        out_shape=shape(SLAB_BLOCKS, BS, KR, dtype=BF16),
        in_specs=[VMEM] * 4,
        out_specs=VMEM,
        compiler_params=pltpu.CompilerParams(vmem_limit_bytes=8 << 20),
    )(*shards)
    near_t = core_swapped(basis_t)
    far_t = far_swapped(basis_t)
    window = pl.pallas_call(
        slots_kernel,
        out_shape=shape(WINDOW + 1, BS, KR),
        in_specs=[SMEM] + [VMEM] * 4 + [pl.BlockSpec(memory_space=pl.ANY)],
        out_specs=VMEM,
        scratch_shapes=[
            pltpu.VMEM((SLAB_BLOCKS, BS, KR), BF16),
            pltpu.VMEM((NNZ_DEV, BS, BS), BF16),
            pltpu.SemaphoreType.DMA((NNZ_DEV // GROUP,)),
        ],
        compiler_params=pltpu.CompilerParams(vmem_limit_bytes=50 << 20),
    )(codes, *shards, tangent.reshape(NNZ_DEV, BS, BS))
    half = KR // 2
    kept, given, near, far = pl.pallas_call(
        gram_kernel,
        out_shape=(shape(half, KR), shape(half, KR), shape(SLAB_BLOCKS, BS, KR), shape(SLAB_BLOCKS, BS, KR)),
        in_specs=[VMEM] * 4,
        out_specs=(VMEM,) * 4,
        compiler_params=pltpu.CompilerParams(vmem_limit_bytes=16 << 20),
    )(window, near_t, basis_t, far_t)

    term = kept + core_swapped(given)
    far_part = far_swapped(far)
    near_part = core_swapped(near)
    term = term + turned(term, "grp", 1) + turned(term, "grp", 2) + turned(term, "grp", 3)
    pieces = pl.pallas_call(
        pieces_kernel,
        out_shape=(shape(VB_DEV, BS, KR),) * 4,
        in_specs=[VMEM] * 3,
        out_specs=(VMEM,) * 4,
        compiler_params=pltpu.CompilerParams(vmem_limit_bytes=16 << 20),
    )(window, near_part, far_part)
    term = term + y_turned(term, 1) + y_turned(term, 2) + y_turned(term, 3)
    received = [turned(pieces[steps], "grp", steps) for steps in (1, 2, 3)]
    term = term + z_paired(term, lambda z: z ^ 1)
    term = term + z_paired(term, lambda z: z ^ 2)
    term, *received = lax.optimization_barrier((term, *received))
    owned_sum = pieces[0] + received[0] + received[1] + received[2]
    term = term + z_paired(term, lambda z: 7 - z)
    term = term * (1.0 / math.sqrt(VB_DEV * BS * GRP * lax.axis_size("row")))
    other = core_swapped(term)
    gram = jnp.where(core == 0, jnp.concatenate([term, other]), jnp.concatenate([other, term]))
    images = owned_sum.astype(BF16).reshape(1, VB_DEV * BS, KR)
    return (images, gram)


def solution(mesh):
    return jax.shard_map(
        body,
        mesh=mesh,
        in_specs=(
            P("row", "grp", None),
            P("row", "grp", None, None),
            P("row", "grp"),
            P("row", "grp"),
            P("row", "grp"),
        ),
        out_specs=(P("row", "grp", None), P()),
        check_vma=False,
    )
```

```python
import math

import jax
import jax.numpy as jnp
from jax import lax
from jax.experimental import pallas as pl
from jax.experimental.pallas import tpu as pltpu
from jax.sharding import PartitionSpec as P

BS = 128
KR = 128
VB_DEV = 4
NNZ_DEV = 288
GRP = 4
SLAB_BLOCKS = VB_DEV * GRP
WINDOW = 3 * SLAB_BLOCKS
GROUP = 48
F32 = jnp.float32
BF16 = jnp.bfloat16
VMEM = pl.BlockSpec(memory_space=pltpu.VMEM)
SMEM = pl.BlockSpec(memory_space=pltpu.SMEM)


def turned(value, axis, steps):
    count = lax.axis_size(axis)
    return lax.ppermute(value, axis, [(source, (source + steps) % count) for source in range(count)])


def row_moved(value, target):
    return lax.ppermute(value, "row", [(source, target(source)) for source in range(64)])


def core_swapped(value):
    return row_moved(value, lambda r: r ^ 1)


def far_swapped(value):
    return lax.ppermute(value, "row", [(r, r + 1 if r % 2 else r - 1) for r in range(1, 63)])


def y_turned(value, steps):
    return row_moved(value, lambda r: r // 8 * 8 + (r // 2 + steps) % 4 * 2 + r % 2)


def z_paired(value, target):
    return row_moved(value, lambda r: target(r // 8) * 8 + r % 8)


def stay_kernel(own, held):
    held[...] = own[...]


def turn_kernel(own, one, two, three, basis_t):
    place = lax.axis_index("grp")
    for steps, shard in enumerate((own, one, two, three)):
        at = (place - steps) & (GRP - 1)
        for block in range(VB_DEV):
            basis_t[at * VB_DEV + block] = shard[pl.ds(block * BS, BS), :].T


def slots_kernel(codes, own, one, two, three, tangent, window, basis, held, sems):
    place = lax.axis_index("grp")
    groups = (codes[0, NNZ_DEV] + GROUP - 1) // GROUP

    def copy(index):
        part = pl.ds(index * GROUP, GROUP)
        return pltpu.make_async_copy(tangent.at[part], held.at[part], sems.at[index])

    def start(index, carry):
        copy(index).start()
        return carry

    lax.fori_loop(0, groups, start, 0)
    for steps, shard in enumerate((own, one, two, three)):
        at = (place - steps) & (GRP - 1)
        for block in range(VB_DEV):
            basis[at * VB_DEV + block] = shard[pl.ds(block * BS, BS), :]
    window[...] = jnp.zeros_like(window)

    def group(index, carry):
        copy(index).wait()
        for offset in range(GROUP):
            slot = index * GROUP + offset
            code = codes[0, slot]
            window[code // SLAB_BLOCKS] += jnp.dot(
                held[slot], basis[code % SLAB_BLOCKS], preferred_element_type=F32
            )
        return carry

    lax.fori_loop(0, groups, group, 0)


def gram_terms(window, first, basis_t, total):
    for block in range(SLAB_BLOCKS):
        value = window[first + block]
        high = value.astype(BF16)
        low = (value - high.astype(F32)).astype(BF16)
        total += jnp.dot(
            basis_t[block], jnp.concatenate([high, low], axis=1), preferred_element_type=F32
        )
    return total


def cut_kernel(window, near, far):
    core = lax.axis_index("row") & 1
    for block in range(SLAB_BLOCKS):
        near[block] = window[(1 - core) * (2 * SLAB_BLOCKS) + block]
        far[block] = window[core * (2 * SLAB_BLOCKS) + block]


def gram_kernel(window, near_t, own_t, far_t, kept, given):
    core = lax.axis_index("row") & 1
    total = jnp.zeros((KR, 2 * KR), F32)
    total = gram_terms(window, SLAB_BLOCKS, own_t, total)
    total = gram_terms(window, (1 - core) * (2 * SLAB_BLOCKS), near_t, total)
    total = gram_terms(window, core * (2 * SLAB_BLOCKS), far_t, total)
    gram = total[:, :KR] + total[:, KR:]
    half = KR // 2
    first = core == 0
    kept[...] = jnp.where(first, gram[:half], gram[half:])
    given[...] = jnp.where(first, gram[half:], gram[:half])


def pieces_kernel(window, near, far, own, one, two, three):
    place = lax.axis_index("grp")
    for steps, piece in enumerate((own, one, two, three)):
        at = ((place + steps) & (GRP - 1)) * VB_DEV
        for block in range(VB_DEV):
            piece[block] = window[SLAB_BLOCKS + at + block] + near[at + block] + far[at + block]


def shape(*sizes, dtype=F32):
    return jax.ShapeDtypeStruct(sizes, dtype)


def body(vectors, tangent, block_cols, dest_blocks, live_slots):
    core = lax.axis_index("row") % 2
    own = vectors.reshape(VB_DEV * BS, KR)
    shards = [turned(own, "grp", steps) for steps in (1, 2, 3)]

    window_base = (lax.axis_index("row") - 1) * SLAB_BLOCKS
    live = lax.broadcasted_iota(jnp.int32, (1, NNZ_DEV), 1) < live_slots
    places = jnp.where(live, dest_blocks - window_base, WINDOW)
    codes = places * SLAB_BLOCKS + (block_cols & (SLAB_BLOCKS - 1))
    codes = jnp.concatenate([codes, live_slots], axis=1)
    own = pl.pallas_call(
        stay_kernel,
        out_shape=shape(VB_DEV * BS, KR, dtype=BF16),
        in_specs=[VMEM],
        out_specs=VMEM,
        compiler_params=pltpu.CompilerParams(vmem_limit_bytes=8 << 20),
    )(own)
    codes, *shards = lax.optimization_barrier((codes, own, *shards))

    basis_t = pl.pallas_call(
        turn_kernel,
        out_shape=shape(SLAB_BLOCKS, BS, KR, dtype=BF16),
        in_specs=[VMEM] * 4,
        out_specs=VMEM,
        compiler_params=pltpu.CompilerParams(vmem_limit_bytes=8 << 20),
    )(*shards)
    near_t = core_swapped(basis_t)
    far_t = far_swapped(basis_t)
    window = pl.pallas_call(
        slots_kernel,
        out_shape=shape(WINDOW + 1, BS, KR),
        in_specs=[SMEM] + [VMEM] * 4 + [pl.BlockSpec(memory_space=pl.ANY)],
        out_specs=VMEM,
        scratch_shapes=[
            pltpu.VMEM((SLAB_BLOCKS, BS, KR), BF16),
            pltpu.VMEM((NNZ_DEV, BS, BS), BF16),
            pltpu.SemaphoreType.DMA((NNZ_DEV // GROUP,)),
        ],
        compiler_params=pltpu.CompilerParams(vmem_limit_bytes=50 << 20),
        cost_estimate=pl.CostEstimate(
            flops=2 * NNZ_DEV * BS * BS * KR, bytes_accessed=2 * NNZ_DEV * BS * BS, transcendentals=0
        ),
    )(codes, *shards, tangent.reshape(NNZ_DEV, BS, BS))
    near, far = pl.pallas_call(
        cut_kernel,
        out_shape=(shape(SLAB_BLOCKS, BS, KR),) * 2,
        in_specs=[VMEM],
        out_specs=(VMEM,) * 2,
        compiler_params=pltpu.CompilerParams(vmem_limit_bytes=16 << 20),
    )(window)
    far_part = far_swapped(far)
    near_part = core_swapped(near)
    half = KR // 2
    kept, given = pl.pallas_call(
        gram_kernel,
        out_shape=(shape(half, KR),) * 2,
        in_specs=[VMEM] * 4,
        out_specs=(VMEM,) * 2,
        compiler_params=pltpu.CompilerParams(vmem_limit_bytes=16 << 20),
    )(window, near_t, basis_t, far_t)

    term = kept + core_swapped(given)
    term = term + turned(term, "grp", 1) + turned(term, "grp", 2) + turned(term, "grp", 3)
    pieces = pl.pallas_call(
        pieces_kernel,
        out_shape=(shape(VB_DEV, BS, KR),) * 4,
        in_specs=[VMEM] * 3,
        out_specs=(VMEM,) * 4,
        compiler_params=pltpu.CompilerParams(vmem_limit_bytes=16 << 20),
    )(window, near_part, far_part)
    term = term + y_turned(term, 1) + y_turned(term, 2) + y_turned(term, 3)
    term, *pieces = lax.optimization_barrier((term, *pieces))
    received = [turned(pieces[steps], "grp", steps) for steps in (1, 2, 3)]
    term = term + z_paired(term, lambda z: z ^ 1)
    term = term + z_paired(term, lambda z: z ^ 2)
    owned_sum = pieces[0] + received[0] + received[1] + received[2]
    term = term + z_paired(term, lambda z: 7 - z)
    term, *received = lax.optimization_barrier((term, *received))
    term = term * (1.0 / math.sqrt(VB_DEV * BS * GRP * lax.axis_size("row")))
    images = owned_sum.astype(BF16).reshape(1, VB_DEV * BS, KR)
    other = core_swapped(term)
    gram = jnp.where(core == 0, jnp.concatenate([term, other]), jnp.concatenate([other, term]))
    return (images, gram)


def solution(mesh):
    return jax.shard_map(
        body,
        mesh=mesh,
        in_specs=(
            P("row", "grp", None),
            P("row", "grp", None, None),
            P("row", "grp"),
            P("row", "grp"),
            P("row", "grp"),
        ),
        out_specs=(P("row", "grp", None), P()),
        check_vma=False,
    )
```

```python
import math

import jax
import jax.numpy as jnp
from jax import lax
from jax.experimental import pallas as pl
from jax.experimental.pallas import tpu as pltpu
from jax.sharding import PartitionSpec as P

BS = 128
KR = 128
VB_DEV = 4
NNZ_DEV = 288
GRP = 4
SLAB_BLOCKS = VB_DEV * GRP
WINDOW = 3 * SLAB_BLOCKS
GROUP = 48
F32 = jnp.float32
BF16 = jnp.bfloat16
VMEM = pl.BlockSpec(memory_space=pltpu.VMEM)
SMEM = pl.BlockSpec(memory_space=pltpu.SMEM)


def turned(value, axis, steps):
    count = lax.axis_size(axis)
    return lax.ppermute(value, axis, [(source, (source + steps) % count) for source in range(count)])


def row_moved(value, target):
    return lax.ppermute(value, "row", [(source, target(source)) for source in range(64)])


def core_swapped(value):
    return row_moved(value, lambda r: r ^ 1)


def far_swapped(value):
    return lax.ppermute(value, "row", [(r, r + 1 if r % 2 else r - 1) for r in range(1, 63)])


def y_turned(value, steps):
    return row_moved(value, lambda r: r // 8 * 8 + (r // 2 + steps) % 4 * 2 + r % 2)


def z_paired(value, target):
    return row_moved(value, lambda r: target(r // 8) * 8 + r % 8)


def stay_kernel(own, held):
    held[...] = own[...]


def turn_kernel(own, one, two, three, basis_t):
    place = lax.axis_index("grp")
    for steps, shard in enumerate((own, one, two, three)):
        at = (place - steps) & (GRP - 1)
        for block in range(VB_DEV):
            basis_t[at * VB_DEV + block] = shard[pl.ds(block * BS, BS), :].T


def slots_kernel(codes, own, one, two, three, tangent, window, basis, held, sems):
    place = lax.axis_index("grp")
    groups = (codes[0, NNZ_DEV] + GROUP - 1) // GROUP

    def copy(index):
        part = pl.ds(index * GROUP, GROUP)
        return pltpu.make_async_copy(tangent.at[part], held.at[part], sems.at[index])

    def start(index, carry):
        copy(index).start()
        return carry

    lax.fori_loop(0, groups, start, 0)
    for steps, shard in enumerate((own, one, two, three)):
        at = (place - steps) & (GRP - 1)
        for block in range(VB_DEV):
            basis[at * VB_DEV + block] = shard[pl.ds(block * BS, BS), :]
    window[...] = jnp.zeros_like(window)

    def group(index, carry):
        copy(index).wait()
        for offset in range(GROUP):
            slot = index * GROUP + offset
            code = codes[0, slot]
            window[code // SLAB_BLOCKS] += jnp.dot(
                held[slot], basis[code % SLAB_BLOCKS], preferred_element_type=F32
            )
        return carry

    lax.fori_loop(0, groups, group, 0)


def gram_terms(window, first, basis_t, total):
    for block in range(SLAB_BLOCKS):
        value = window[first + block]
        high = value.astype(BF16)
        low = (value - high.astype(F32)).astype(BF16)
        total += jnp.dot(
            basis_t[block], jnp.concatenate([high, low], axis=1), preferred_element_type=F32
        )
    return total


def cut_kernel(window, near, far):
    core = lax.axis_index("row") & 1
    for block in range(SLAB_BLOCKS):
        near[block] = window[(1 - core) * (2 * SLAB_BLOCKS) + block]
        far[block] = window[core * (2 * SLAB_BLOCKS) + block]


def gram_kernel(window, near_t, own_t, far_t, kept, given):
    core = lax.axis_index("row") & 1
    total = jnp.zeros((KR, 2 * KR), F32)
    total = gram_terms(window, SLAB_BLOCKS, own_t, total)
    total = gram_terms(window, (1 - core) * (2 * SLAB_BLOCKS), near_t, total)
    total = gram_terms(window, core * (2 * SLAB_BLOCKS), far_t, total)
    gram = total[:, :KR] + total[:, KR:]
    half = KR // 2
    first = core == 0
    kept[...] = jnp.where(first, gram[:half], gram[half:])
    given[...] = jnp.where(first, gram[half:], gram[:half])


def pieces_kernel(window, near, far, own, one, two, three):
    place = lax.axis_index("grp")
    for steps, piece in enumerate((own, one, two, three)):
        at = ((place + steps) & (GRP - 1)) * VB_DEV
        for block in range(VB_DEV):
            piece[block] = window[SLAB_BLOCKS + at + block] + near[at + block] + far[at + block]


def shape(*sizes, dtype=F32):
    return jax.ShapeDtypeStruct(sizes, dtype)


def body(vectors, tangent, block_cols, dest_blocks, live_slots):
    core = lax.axis_index("row") % 2
    own = vectors.reshape(VB_DEV * BS, KR)
    shards = [turned(own, "grp", steps) for steps in (1, 2, 3)]

    window_base = (lax.axis_index("row") - 1) * SLAB_BLOCKS
    live = lax.broadcasted_iota(jnp.int32, (1, NNZ_DEV), 1) < live_slots
    places = jnp.where(live, dest_blocks - window_base, WINDOW)
    codes = places * SLAB_BLOCKS + (block_cols & (SLAB_BLOCKS - 1))
    codes = jnp.concatenate([codes, live_slots], axis=1)
    own = pl.pallas_call(
        stay_kernel,
        out_shape=shape(VB_DEV * BS, KR, dtype=BF16),
        in_specs=[VMEM],
        out_specs=VMEM,
        compiler_params=pltpu.CompilerParams(vmem_limit_bytes=8 << 20),
    )(own)
    codes, *shards = lax.optimization_barrier((codes, own, *shards))

    basis_t = pl.pallas_call(
        turn_kernel,
        out_shape=shape(SLAB_BLOCKS, BS, KR, dtype=BF16),
        in_specs=[VMEM] * 4,
        out_specs=VMEM,
        compiler_params=pltpu.CompilerParams(vmem_limit_bytes=8 << 20),
    )(*shards)
    near_t = core_swapped(basis_t)
    far_t = far_swapped(basis_t)
    window = pl.pallas_call(
        slots_kernel,
        out_shape=shape(WINDOW + 1, BS, KR),
        in_specs=[SMEM] + [VMEM] * 4 + [pl.BlockSpec(memory_space=pl.ANY)],
        out_specs=VMEM,
        scratch_shapes=[
            pltpu.VMEM((SLAB_BLOCKS, BS, KR), BF16),
            pltpu.VMEM((NNZ_DEV, BS, BS), BF16),
            pltpu.SemaphoreType.DMA((NNZ_DEV // GROUP,)),
        ],
        compiler_params=pltpu.CompilerParams(vmem_limit_bytes=50 << 20),
        cost_estimate=pl.CostEstimate(
            flops=2 * NNZ_DEV * BS * BS * KR, bytes_accessed=2 * NNZ_DEV * BS * BS, transcendentals=0
        ),
    )(codes, *shards, tangent.reshape(NNZ_DEV, BS, BS))
    near, far = pl.pallas_call(
        cut_kernel,
        out_shape=(shape(SLAB_BLOCKS, BS, KR),) * 2,
        in_specs=[VMEM],
        out_specs=(VMEM,) * 2,
        compiler_params=pltpu.CompilerParams(vmem_limit_bytes=16 << 20),
    )(window)
    far_part = far_swapped(far)
    near_part = core_swapped(near)
    half = KR // 2
    kept, given = pl.pallas_call(
        gram_kernel,
        out_shape=(shape(half, KR),) * 2,
        in_specs=[VMEM] * 4,
        out_specs=(VMEM,) * 2,
        compiler_params=pltpu.CompilerParams(vmem_limit_bytes=16 << 20),
        cost_estimate=pl.CostEstimate(
            flops=64 * WINDOW * BS * KR * KR, bytes_accessed=96 * WINDOW * BS * KR, transcendentals=0
        ),
    )(window, near_t, basis_t, far_t)

    term = kept + core_swapped(given)
    term = term + turned(term, "grp", 1) + turned(term, "grp", 2) + turned(term, "grp", 3)
    pieces = pl.pallas_call(
        pieces_kernel,
        out_shape=(shape(VB_DEV, BS, KR),) * 4,
        in_specs=[VMEM] * 3,
        out_specs=(VMEM,) * 4,
        compiler_params=pltpu.CompilerParams(vmem_limit_bytes=16 << 20),
    )(window, near_part, far_part)
    term = term + y_turned(term, 1) + y_turned(term, 2) + y_turned(term, 3)
    received = [turned(pieces[steps], "grp", steps) for steps in (1, 2, 3)]
    term = term + z_paired(term, lambda z: z ^ 1)
    term = term + z_paired(term, lambda z: z ^ 2)
    owned_sum = pieces[0] + received[0] + received[1] + received[2]
    term = term + z_paired(term, lambda z: 7 - z)
    term, *received = lax.optimization_barrier((term, *received))
    term = term * (1.0 / math.sqrt(VB_DEV * BS * GRP * lax.axis_size("row")))
    images = owned_sum.astype(BF16).reshape(1, VB_DEV * BS, KR)
    other = core_swapped(term)
    gram = jnp.where(core == 0, jnp.concatenate([term, other]), jnp.concatenate([other, term]))
    return (images, gram)


def solution(mesh):
    return jax.shard_map(
        body,
        mesh=mesh,
        in_specs=(
            P("row", "grp", None),
            P("row", "grp", None, None),
            P("row", "grp"),
            P("row", "grp"),
            P("row", "grp"),
        ),
        out_specs=(P("row", "grp", None), P()),
        check_vma=False,
    )
```

```python
import math

import jax
import jax.numpy as jnp
from jax import lax
from jax.experimental import pallas as pl
from jax.experimental.pallas import tpu as pltpu
from jax.sharding import PartitionSpec as P

BS = 128
KR = 128
VB_DEV = 4
NNZ_DEV = 288
GRP = 4
SLAB_BLOCKS = VB_DEV * GRP
WINDOW = 3 * SLAB_BLOCKS
GROUP = 48
F32 = jnp.float32
BF16 = jnp.bfloat16
VMEM = pl.BlockSpec(memory_space=pltpu.VMEM)
SMEM = pl.BlockSpec(memory_space=pltpu.SMEM)


def turned(value, axis, steps):
    count = lax.axis_size(axis)
    return lax.ppermute(value, axis, [(source, (source + steps) % count) for source in range(count)])


def row_moved(value, target):
    return lax.ppermute(value, "row", [(source, target(source)) for source in range(64)])


def core_swapped(value):
    return row_moved(value, lambda r: r ^ 1)


def far_swapped(value):
    return lax.ppermute(value, "row", [(r, r + 1 if r % 2 else r - 1) for r in range(1, 63)])


def y_turned(value, steps):
    return row_moved(value, lambda r: r // 8 * 8 + (r // 2 + steps) % 4 * 2 + r % 2)


def z_paired(value, target):
    return row_moved(value, lambda r: target(r // 8) * 8 + r % 8)


def stay_kernel(own, held):
    held[...] = own[...]


def turn_kernel(own, one, two, three, basis_t):
    place = lax.axis_index("grp")
    for steps, shard in enumerate((own, one, two, three)):
        at = (place - steps) & (GRP - 1)
        for block in range(VB_DEV):
            basis_t[at * VB_DEV + block] = shard[pl.ds(block * BS, BS), :].T


def slots_kernel(codes, own, one, two, three, tangent, window, basis, held, sems):
    place = lax.axis_index("grp")
    groups = (codes[0, NNZ_DEV] + GROUP - 1) // GROUP

    def copy(index):
        part = pl.ds(index * GROUP, GROUP)
        return pltpu.make_async_copy(tangent.at[part], held.at[part], sems.at[index])

    def start(index, carry):
        copy(index).start()
        return carry

    lax.fori_loop(0, groups, start, 0)
    for steps, shard in enumerate((own, one, two, three)):
        at = (place - steps) & (GRP - 1)
        for block in range(VB_DEV):
            basis[at * VB_DEV + block] = shard[pl.ds(block * BS, BS), :]
    window[...] = jnp.zeros_like(window)

    def group(index, carry):
        copy(index).wait()
        for offset in range(GROUP):
            slot = index * GROUP + offset
            code = codes[0, slot]
            window[code // SLAB_BLOCKS] += jnp.dot(
                held[slot], basis[code % SLAB_BLOCKS], preferred_element_type=F32
            )
        return carry

    lax.fori_loop(0, groups, group, 0)


def gram_terms(window, first, basis_t, total):
    for block in range(SLAB_BLOCKS):
        value = window[first + block]
        high = value.astype(BF16)
        low = (value - high.astype(F32)).astype(BF16)
        total += jnp.dot(
            basis_t[block], jnp.concatenate([high, low], axis=1), preferred_element_type=F32
        )
    return total


def cut_kernel(window, near, far):
    core = lax.axis_index("row") & 1
    for block in range(SLAB_BLOCKS):
        near[block] = window[(1 - core) * (2 * SLAB_BLOCKS) + block]
        far[block] = window[core * (2 * SLAB_BLOCKS) + block]


def gram_kernel(window, near_t, own_t, far_t, kept, given):
    core = lax.axis_index("row") & 1
    total = jnp.zeros((KR, 2 * KR), F32)
    total = gram_terms(window, SLAB_BLOCKS, own_t, total)
    total = gram_terms(window, (1 - core) * (2 * SLAB_BLOCKS), near_t, total)
    total = gram_terms(window, core * (2 * SLAB_BLOCKS), far_t, total)
    gram = total[:, :KR] + total[:, KR:]
    half = KR // 2
    first = core == 0
    kept[...] = jnp.where(first, gram[:half], gram[half:])
    given[...] = jnp.where(first, gram[half:], gram[:half])


def pieces_kernel(window, near, far, own, one, two, three):
    place = lax.axis_index("grp")
    for steps, piece in enumerate((own, one, two, three)):
        at = ((place + steps) & (GRP - 1)) * VB_DEV
        for block in range(VB_DEV):
            piece[block] = window[SLAB_BLOCKS + at + block] + near[at + block] + far[at + block]


def shape(*sizes, dtype=F32):
    return jax.ShapeDtypeStruct(sizes, dtype)


def body(vectors, tangent, block_cols, dest_blocks, live_slots):
    core = lax.axis_index("row") % 2
    own = vectors.reshape(VB_DEV * BS, KR)
    shards = [turned(own, "grp", steps) for steps in (1, 2, 3)]

    window_base = (lax.axis_index("row") - 1) * SLAB_BLOCKS
    live = lax.broadcasted_iota(jnp.int32, (1, NNZ_DEV), 1) < live_slots
    places = jnp.where(live, dest_blocks - window_base, WINDOW)
    codes = places * SLAB_BLOCKS + (block_cols & (SLAB_BLOCKS - 1))
    codes = jnp.concatenate([codes, live_slots], axis=1)
    own = pl.pallas_call(
        stay_kernel,
        out_shape=shape(VB_DEV * BS, KR, dtype=BF16),
        in_specs=[VMEM],
        out_specs=VMEM,
        compiler_params=pltpu.CompilerParams(vmem_limit_bytes=8 << 20),
    )(own)
    codes, *shards = lax.optimization_barrier((codes, own, *shards))

    basis_t = pl.pallas_call(
        turn_kernel,
        out_shape=shape(SLAB_BLOCKS, BS, KR, dtype=BF16),
        in_specs=[VMEM] * 4,
        out_specs=VMEM,
        compiler_params=pltpu.CompilerParams(vmem_limit_bytes=8 << 20),
    )(*shards)
    near_t = core_swapped(basis_t)
    far_t = far_swapped(basis_t)
    window = pl.pallas_call(
        slots_kernel,
        out_shape=shape(WINDOW + 1, BS, KR),
        in_specs=[SMEM] + [VMEM] * 4 + [pl.BlockSpec(memory_space=pl.ANY)],
        out_specs=VMEM,
        scratch_shapes=[
            pltpu.VMEM((SLAB_BLOCKS, BS, KR), BF16),
            pltpu.VMEM((NNZ_DEV, BS, BS), BF16),
            pltpu.SemaphoreType.DMA((NNZ_DEV // GROUP,)),
        ],
        compiler_params=pltpu.CompilerParams(vmem_limit_bytes=50 << 20),
        cost_estimate=pl.CostEstimate(
            flops=2 * NNZ_DEV * BS * BS * KR, bytes_accessed=2 * NNZ_DEV * BS * BS, transcendentals=0
        ),
    )(codes, *shards, tangent.reshape(NNZ_DEV, BS, BS))
    near, far = pl.pallas_call(
        cut_kernel,
        out_shape=(shape(SLAB_BLOCKS, BS, KR),) * 2,
        in_specs=[VMEM],
        out_specs=(VMEM,) * 2,
        compiler_params=pltpu.CompilerParams(vmem_limit_bytes=16 << 20),
    )(window)
    far_part = far_swapped(far)
    near_part = core_swapped(near)
    half = KR // 2
    kept, given = pl.pallas_call(
        gram_kernel,
        out_shape=(shape(half, KR),) * 2,
        in_specs=[VMEM] * 4,
        out_specs=(VMEM,) * 2,
        compiler_params=pltpu.CompilerParams(vmem_limit_bytes=16 << 20),
        cost_estimate=pl.CostEstimate(
            flops=64 * WINDOW * BS * KR * KR, bytes_accessed=96 * WINDOW * BS * KR, transcendentals=0
        ),
    )(window, near_t, basis_t, far_t)

    term = kept + core_swapped(given)
    term = term + turned(term, "grp", 1) + turned(term, "grp", 2) + turned(term, "grp", 3)
    pieces = pl.pallas_call(
        pieces_kernel,
        out_shape=(shape(VB_DEV, BS, KR),) * 4,
        in_specs=[VMEM] * 3,
        out_specs=(VMEM,) * 4,
        compiler_params=pltpu.CompilerParams(vmem_limit_bytes=16 << 20),
    )(window, near_part, far_part)
    term = term + y_turned(term, 1) + y_turned(term, 2) + y_turned(term, 3)
    received = [turned(pieces[steps], "grp", steps) for steps in (1, 2, 3)]
    term = term + z_paired(term, lambda z: z ^ 1)
    term = term + z_paired(term, lambda z: z ^ 2)
    owned_sum = pieces[0] + received[0] + received[1] + received[2]
    term = term + z_paired(term, lambda z: z ^ 6)
    term, *received = lax.optimization_barrier((term, *received))
    term = term * (1.0 / math.sqrt(VB_DEV * BS * GRP * lax.axis_size("row")))
    images = owned_sum.astype(BF16).reshape(1, VB_DEV * BS, KR)
    other = core_swapped(term)
    gram = jnp.where(core == 0, jnp.concatenate([term, other]), jnp.concatenate([other, term]))
    return (images, gram)


def solution(mesh):
    return jax.shard_map(
        body,
        mesh=mesh,
        in_specs=(
            P("row", "grp", None),
            P("row", "grp", None, None),
            P("row", "grp"),
            P("row", "grp"),
            P("row", "grp"),
        ),
        out_specs=(P("row", "grp", None), P()),
        check_vma=False,
    )
```

```python
import math

import jax
import jax.numpy as jnp
from jax import lax
from jax.experimental import pallas as pl
from jax.experimental.pallas import tpu as pltpu
from jax.sharding import PartitionSpec as P

BS = 128
KR = 128
VB_DEV = 4
NNZ_DEV = 288
GRP = 4
SLAB_BLOCKS = VB_DEV * GRP
WINDOW = 3 * SLAB_BLOCKS
GROUP = 48
F32 = jnp.float32
BF16 = jnp.bfloat16
VMEM = pl.BlockSpec(memory_space=pltpu.VMEM)
SMEM = pl.BlockSpec(memory_space=pltpu.SMEM)


def turned(value, axis, steps):
    count = lax.axis_size(axis)
    return lax.ppermute(value, axis, [(source, (source + steps) % count) for source in range(count)])


def row_moved(value, target):
    return lax.ppermute(value, "row", [(source, target(source)) for source in range(64)])


def core_swapped(value):
    return row_moved(value, lambda r: r ^ 1)


def far_swapped(value):
    return lax.ppermute(value, "row", [(r, r + 1 if r % 2 else r - 1) for r in range(1, 63)])


def y_turned(value, steps):
    return row_moved(value, lambda r: r // 8 * 8 + (r // 2 + steps) % 4 * 2 + r % 2)


def z_paired(value, target):
    return row_moved(value, lambda r: target(r // 8) * 8 + r % 8)


def stay_kernel(own, held):
    held[...] = own[...]


def turn_kernel(own, one, two, three, basis_t):
    place = lax.axis_index("grp")
    for steps, shard in enumerate((own, one, two, three)):
        at = (place - steps) & (GRP - 1)
        for block in range(VB_DEV):
            basis_t[at * VB_DEV + block] = shard[pl.ds(block * BS, BS), :].T


def slots_kernel(codes, own, one, two, three, tangent, window, basis, held, sems):
    place = lax.axis_index("grp")
    groups = (codes[0, NNZ_DEV] + GROUP - 1) // GROUP

    def copy(index):
        part = pl.ds(index * GROUP, GROUP)
        return pltpu.make_async_copy(tangent.at[part], held.at[part], sems.at[index])

    def start(index, carry):
        copy(index).start()
        return carry

    lax.fori_loop(0, groups, start, 0)
    for steps, shard in enumerate((own, one, two, three)):
        at = (place - steps) & (GRP - 1)
        for block in range(VB_DEV):
            basis[at * VB_DEV + block] = shard[pl.ds(block * BS, BS), :]
    window[...] = jnp.zeros_like(window)

    def group(index, carry):
        copy(index).wait()
        for offset in range(GROUP):
            slot = index * GROUP + offset
            code = codes[0, slot]
            window[code // SLAB_BLOCKS] += jnp.dot(
                held[slot], basis[code % SLAB_BLOCKS], preferred_element_type=F32
            )
        return carry

    lax.fori_loop(0, groups, group, 0)


def gram_terms(window, first, basis_t, total):
    for block in range(SLAB_BLOCKS):
        value = window[first + block]
        high = value.astype(BF16)
        low = (value - high.astype(F32)).astype(BF16)
        total += jnp.dot(
            basis_t[block], jnp.concatenate([high, low], axis=1), preferred_element_type=F32
        )
    return total


def cut_kernel(window, near, far):
    core = lax.axis_index("row") & 1
    for block in range(SLAB_BLOCKS):
        near[block] = window[(1 - core) * (2 * SLAB_BLOCKS) + block]
        far[block] = window[core * (2 * SLAB_BLOCKS) + block]


def gram_kernel(window, near_t, own_t, far_t, kept, given):
    core = lax.axis_index("row") & 1
    total = jnp.zeros((KR, 2 * KR), F32)
    total = gram_terms(window, SLAB_BLOCKS, own_t, total)
    total = gram_terms(window, (1 - core) * (2 * SLAB_BLOCKS), near_t, total)
    total = gram_terms(window, core * (2 * SLAB_BLOCKS), far_t, total)
    gram = total[:, :KR] + total[:, KR:]
    half = KR // 2
    first = core == 0
    kept[...] = jnp.where(first, gram[:half], gram[half:])
    given[...] = jnp.where(first, gram[half:], gram[:half])


def pieces_kernel(window, near, far, own, one, two, three):
    place = lax.axis_index("grp")
    for steps, piece in enumerate((own, one, two, three)):
        at = ((place + steps) & (GRP - 1)) * VB_DEV
        for block in range(VB_DEV):
            piece[block] = window[SLAB_BLOCKS + at + block] + near[at + block] + far[at + block]


def shape(*sizes, dtype=F32):
    return jax.ShapeDtypeStruct(sizes, dtype)


def body(vectors, tangent, block_cols, dest_blocks, live_slots):
    core = lax.axis_index("row") % 2
    own = vectors.reshape(VB_DEV * BS, KR)
    shards = [turned(own, "grp", steps) for steps in (1, 2, 3)]

    window_base = (lax.axis_index("row") - 1) * SLAB_BLOCKS
    live = lax.broadcasted_iota(jnp.int32, (1, NNZ_DEV), 1) < live_slots
    places = jnp.where(live, dest_blocks - window_base, WINDOW)
    codes = places * SLAB_BLOCKS + (block_cols & (SLAB_BLOCKS - 1))
    codes = jnp.concatenate([codes, live_slots], axis=1)
    own = pl.pallas_call(
        stay_kernel,
        out_shape=shape(VB_DEV * BS, KR, dtype=BF16),
        in_specs=[VMEM],
        out_specs=VMEM,
        compiler_params=pltpu.CompilerParams(vmem_limit_bytes=8 << 20),
    )(own)
    codes, *shards = lax.optimization_barrier((codes, own, *shards))

    basis_t = pl.pallas_call(
        turn_kernel,
        out_shape=shape(SLAB_BLOCKS, BS, KR, dtype=BF16),
        in_specs=[VMEM] * 4,
        out_specs=VMEM,
        compiler_params=pltpu.CompilerParams(vmem_limit_bytes=8 << 20),
    )(*shards)
    near_t = core_swapped(basis_t)
    far_t = far_swapped(basis_t)
    window = pl.pallas_call(
        slots_kernel,
        out_shape=shape(WINDOW + 1, BS, KR),
        in_specs=[SMEM] + [VMEM] * 4 + [pl.BlockSpec(memory_space=pl.ANY)],
        out_specs=VMEM,
        scratch_shapes=[
            pltpu.VMEM((SLAB_BLOCKS, BS, KR), BF16),
            pltpu.VMEM((NNZ_DEV, BS, BS), BF16),
            pltpu.SemaphoreType.DMA((NNZ_DEV // GROUP,)),
        ],
        compiler_params=pltpu.CompilerParams(vmem_limit_bytes=50 << 20),
        cost_estimate=pl.CostEstimate(
            flops=2 * NNZ_DEV * BS * BS * KR, bytes_accessed=2 * NNZ_DEV * BS * BS, transcendentals=0
        ),
    )(codes, *shards, tangent.reshape(NNZ_DEV, BS, BS))
    near, far = pl.pallas_call(
        cut_kernel,
        out_shape=(shape(SLAB_BLOCKS, BS, KR),) * 2,
        in_specs=[VMEM],
        out_specs=(VMEM,) * 2,
        compiler_params=pltpu.CompilerParams(vmem_limit_bytes=16 << 20),
    )(window)
    far_part = far_swapped(far)
    half = KR // 2
    kept, given = pl.pallas_call(
        gram_kernel,
        out_shape=(shape(half, KR),) * 2,
        in_specs=[VMEM] * 4,
        out_specs=(VMEM,) * 2,
        compiler_params=pltpu.CompilerParams(vmem_limit_bytes=16 << 20),
        cost_estimate=pl.CostEstimate(
            flops=64 * WINDOW * BS * KR * KR, bytes_accessed=96 * WINDOW * BS * KR, transcendentals=0
        ),
    )(window, near_t, basis_t, far_t)

    given, near = lax.optimization_barrier((given, near))
    near_part = core_swapped(near)
    term = kept + core_swapped(given)
    term = term + turned(term, "grp", 1) + turned(term, "grp", 2) + turned(term, "grp", 3)
    pieces = pl.pallas_call(
        pieces_kernel,
        out_shape=(shape(VB_DEV, BS, KR),) * 4,
        in_specs=[VMEM] * 3,
        out_specs=(VMEM,) * 4,
        compiler_params=pltpu.CompilerParams(vmem_limit_bytes=16 << 20),
    )(window, near_part, far_part)
    term = term + y_turned(term, 1) + y_turned(term, 2) + y_turned(term, 3)
    received = [turned(pieces[steps], "grp", steps) for steps in (1, 2, 3)]
    term = term + z_paired(term, lambda z: z ^ 1)
    term = term + z_paired(term, lambda z: z ^ 2)
    owned_sum = pieces[0] + received[0] + received[1] + received[2]
    term = term + z_paired(term, lambda z: 7 - z)
    term, *received = lax.optimization_barrier((term, *received))
    term = term * (1.0 / math.sqrt(VB_DEV * BS * GRP * lax.axis_size("row")))
    images = owned_sum.astype(BF16).reshape(1, VB_DEV * BS, KR)
    other = core_swapped(term)
    gram = jnp.where(core == 0, jnp.concatenate([term, other]), jnp.concatenate([other, term]))
    return (images, gram)


def solution(mesh):
    return jax.shard_map(
        body,
        mesh=mesh,
        in_specs=(
            P("row", "grp", None),
            P("row", "grp", None, None),
            P("row", "grp"),
            P("row", "grp"),
            P("row", "grp"),
        ),
        out_specs=(P("row", "grp", None), P()),
        check_vma=False,
    )
```

```python
import math

import jax
import jax.numpy as jnp
from jax import lax
from jax.experimental import pallas as pl
from jax.experimental.pallas import tpu as pltpu
from jax.sharding import PartitionSpec as P

BS = 128
KR = 128
VB_DEV = 4
NNZ_DEV = 288
GRP = 4
SLAB_BLOCKS = VB_DEV * GRP
WINDOW = 3 * SLAB_BLOCKS
GROUP = 48
F32 = jnp.float32
BF16 = jnp.bfloat16
VMEM = pl.BlockSpec(memory_space=pltpu.VMEM)
SMEM = pl.BlockSpec(memory_space=pltpu.SMEM)


def turned(value, axis, steps):
    count = lax.axis_size(axis)
    return lax.ppermute(value, axis, [(source, (source + steps) % count) for source in range(count)])


def row_moved(value, target):
    return lax.ppermute(value, "row", [(source, target(source)) for source in range(64)])


def core_swapped(value):
    return row_moved(value, lambda r: r ^ 1)


def far_swapped(value):
    return lax.ppermute(value, "row", [(r, r + 1 if r % 2 else r - 1) for r in range(1, 63)])


def y_turned(value, steps):
    return row_moved(value, lambda r: r // 8 * 8 + (r // 2 + steps) % 4 * 2 + r % 2)


def z_paired(value, target):
    return row_moved(value, lambda r: target(r // 8) * 8 + r % 8)


def stay_kernel(own, held):
    held[...] = own[...]


def turn_kernel(own, one, two, three, basis_t):
    place = lax.axis_index("grp")
    for steps, shard in enumerate((own, one, two, three)):
        at = (place - steps) & (GRP - 1)
        for block in range(VB_DEV):
            basis_t[at * VB_DEV + block] = shard[pl.ds(block * BS, BS), :].T


def slots_kernel(codes, own, one, two, three, tangent, window, basis, held, sems):
    place = lax.axis_index("grp")
    groups = (codes[0, NNZ_DEV] + GROUP - 1) // GROUP

    def copy(index):
        part = pl.ds(index * GROUP, GROUP)
        return pltpu.make_async_copy(tangent.at[part], held.at[part], sems.at[index])

    def start(index):
        @pl.when(index < groups)
        def _():
            copy(index).start()

    start(0)
    start(1)
    for steps, shard in enumerate((own, one, two, three)):
        at = (place - steps) & (GRP - 1)
        for block in range(VB_DEV):
            basis[at * VB_DEV + block] = shard[pl.ds(block * BS, BS), :]
    window[...] = jnp.zeros_like(window)

    def group(index, carry):
        copy(index).wait()
        start(index + 2)
        for offset in range(GROUP):
            slot = index * GROUP + offset
            code = codes[0, slot]
            window[code // SLAB_BLOCKS] += jnp.dot(
                held[slot], basis[code % SLAB_BLOCKS], preferred_element_type=F32
            )
        return carry

    lax.fori_loop(0, groups, group, 0)


def gram_terms(window, first, basis_t, total):
    for block in range(SLAB_BLOCKS):
        value = window[first + block]
        high = value.astype(BF16)
        low = (value - high.astype(F32)).astype(BF16)
        total += jnp.dot(
            basis_t[block], jnp.concatenate([high, low], axis=1), preferred_element_type=F32
        )
    return total


def cut_kernel(window, near, far):
    core = lax.axis_index("row") & 1
    for block in range(SLAB_BLOCKS):
        near[block] = window[(1 - core) * (2 * SLAB_BLOCKS) + block]
        far[block] = window[core * (2 * SLAB_BLOCKS) + block]


def gram_kernel(window, near_t, own_t, far_t, kept, given):
    core = lax.axis_index("row") & 1
    total = jnp.zeros((KR, 2 * KR), F32)
    total = gram_terms(window, SLAB_BLOCKS, own_t, total)
    total = gram_terms(window, (1 - core) * (2 * SLAB_BLOCKS), near_t, total)
    total = gram_terms(window, core * (2 * SLAB_BLOCKS), far_t, total)
    gram = total[:, :KR] + total[:, KR:]
    half = KR // 2
    first = core == 0
    kept[...] = jnp.where(first, gram[:half], gram[half:])
    given[...] = jnp.where(first, gram[half:], gram[:half])


def pieces_kernel(window, near, far, own, one, two, three):
    place = lax.axis_index("grp")
    for steps, piece in enumerate((own, one, two, three)):
        at = ((place + steps) & (GRP - 1)) * VB_DEV
        for block in range(VB_DEV):
            piece[block] = window[SLAB_BLOCKS + at + block] + near[at + block] + far[at + block]


def shape(*sizes, dtype=F32):
    return jax.ShapeDtypeStruct(sizes, dtype)


def body(vectors, tangent, block_cols, dest_blocks, live_slots):
    core = lax.axis_index("row") % 2
    own = vectors.reshape(VB_DEV * BS, KR)
    shards = [turned(own, "grp", steps) for steps in (1, 2, 3)]

    window_base = (lax.axis_index("row") - 1) * SLAB_BLOCKS
    live = lax.broadcasted_iota(jnp.int32, (1, NNZ_DEV), 1) < live_slots
    places = jnp.where(live, dest_blocks - window_base, WINDOW)
    codes = places * SLAB_BLOCKS + (block_cols & (SLAB_BLOCKS - 1))
    codes = jnp.concatenate([codes, live_slots], axis=1)
    own = pl.pallas_call(
        stay_kernel,
        out_shape=shape(VB_DEV * BS, KR, dtype=BF16),
        in_specs=[VMEM],
        out_specs=VMEM,
        compiler_params=pltpu.CompilerParams(vmem_limit_bytes=8 << 20),
    )(own)
    codes, *shards = lax.optimization_barrier((codes, own, *shards))

    basis_t = pl.pallas_call(
        turn_kernel,
        out_shape=shape(SLAB_BLOCKS, BS, KR, dtype=BF16),
        in_specs=[VMEM] * 4,
        out_specs=VMEM,
        compiler_params=pltpu.CompilerParams(vmem_limit_bytes=8 << 20),
    )(*shards)
    near_t = core_swapped(basis_t)
    far_t = far_swapped(basis_t)
    window = pl.pallas_call(
        slots_kernel,
        out_shape=shape(WINDOW + 1, BS, KR),
        in_specs=[SMEM] + [VMEM] * 4 + [pl.BlockSpec(memory_space=pl.ANY)],
        out_specs=VMEM,
        scratch_shapes=[
            pltpu.VMEM((SLAB_BLOCKS, BS, KR), BF16),
            pltpu.VMEM((NNZ_DEV, BS, BS), BF16),
            pltpu.SemaphoreType.DMA((NNZ_DEV // GROUP,)),
        ],
        compiler_params=pltpu.CompilerParams(vmem_limit_bytes=50 << 20),
        cost_estimate=pl.CostEstimate(
            flops=2 * NNZ_DEV * BS * BS * KR, bytes_accessed=2 * NNZ_DEV * BS * BS, transcendentals=0
        ),
    )(codes, *shards, tangent.reshape(NNZ_DEV, BS, BS))
    near, far = pl.pallas_call(
        cut_kernel,
        out_shape=(shape(SLAB_BLOCKS, BS, KR),) * 2,
        in_specs=[VMEM],
        out_specs=(VMEM,) * 2,
        compiler_params=pltpu.CompilerParams(vmem_limit_bytes=16 << 20),
    )(window)
    far_part = far_swapped(far)
    half = KR // 2
    kept, given = pl.pallas_call(
        gram_kernel,
        out_shape=(shape(half, KR),) * 2,
        in_specs=[VMEM] * 4,
        out_specs=(VMEM,) * 2,
        compiler_params=pltpu.CompilerParams(vmem_limit_bytes=16 << 20),
        cost_estimate=pl.CostEstimate(
            flops=64 * WINDOW * BS * KR * KR, bytes_accessed=96 * WINDOW * BS * KR, transcendentals=0
        ),
    )(window, near_t, basis_t, far_t)

    given, near = lax.optimization_barrier((given, near))
    near_part = core_swapped(near)
    term = kept + core_swapped(given)
    term = term + turned(term, "grp", 1) + turned(term, "grp", 2) + turned(term, "grp", 3)
    pieces = pl.pallas_call(
        pieces_kernel,
        out_shape=(shape(VB_DEV, BS, KR),) * 4,
        in_specs=[VMEM] * 3,
        out_specs=(VMEM,) * 4,
        compiler_params=pltpu.CompilerParams(vmem_limit_bytes=16 << 20),
    )(window, near_part, far_part)
    term = term + y_turned(term, 1) + y_turned(term, 2) + y_turned(term, 3)
    received = [turned(pieces[steps], "grp", steps) for steps in (1, 2, 3)]
    term = term + z_paired(term, lambda z: z ^ 1)
    term = term + z_paired(term, lambda z: z ^ 2)
    owned_sum = pieces[0] + received[0] + received[1] + received[2]
    term = term + z_paired(term, lambda z: 7 - z)
    term, *received = lax.optimization_barrier((term, *received))
    term = term * (1.0 / math.sqrt(VB_DEV * BS * GRP * lax.axis_size("row")))
    images = owned_sum.astype(BF16).reshape(1, VB_DEV * BS, KR)
    other = core_swapped(term)
    gram = jnp.where(core == 0, jnp.concatenate([term, other]), jnp.concatenate([other, term]))
    return (images, gram)


def solution(mesh):
    return jax.shard_map(
        body,
        mesh=mesh,
        in_specs=(
            P("row", "grp", None),
            P("row", "grp", None, None),
            P("row", "grp"),
            P("row", "grp"),
            P("row", "grp"),
        ),
        out_specs=(P("row", "grp", None), P()),
        check_vma=False,
    )
```
